512 devices in a mesh: rep: 8 (over x, z_hi), fsdp: 64 (over y, z_lo, core).
Axes of the slice: x: 4, y: 4, z: 16 (z_hi: 2, z_lo: 8; z = z_hi * 8 + z_lo), core: 2. Of those that a mesh axis runs over, the one named last changes fastest.
Arguments:
- tokens: bfloat16 [65536, 4096], P(('rep', 'fsdp')), may hold values from -6 to 6
- kv_weight: bfloat16 [8, 4096, 1024], P('rep', 'fsdp'), may hold values from -0.09375 to 0.09375
- kv_cotangent: bfloat16 [65536, 1024], P(('rep', 'fsdp')), may hold values from -6 to 6
- fragment_index: int32 [1], replicated, may hold values from 0 to 7
- anchor: float32 [8, 262144], P(None, 'fsdp'), may hold values from -6 to 6
- momentum: float32 [8, 262144], P(None, 'fsdp'), may hold values from -6 to 6
- replica_frag: bfloat16 [8, 8, 262144], P('rep', None, 'fsdp'), may hold values from -6 to 6
Outputs:
- key_value: bfloat16 [65536, 1024], P(('rep', 'fsdp'))
- input_grad: bfloat16 [65536, 4096], P(('rep', 'fsdp'))
- anchor_new: float32 [262144], P('fsdp')
- momentum_new: float32 [262144], P('fsdp')
The draws below stay inside these ranges and needn't reach their ends.
All inputs are finite; a program needn't handle non-finite values.
Results may differ from the reference program's by a relative error of at most 0.0049.
Values may be sent and summed in bfloat16 or wider, within the bound.
No kernel may reach another device: no remote copies, remote signals or barrier semaphores. Data moves between devices by JAX's collectives and lax.ppermute only.
A program may use at most 64 MiB of HBM per device.

```python
import jax
import jax.numpy as jnp
from jax import lax

D = 4096
KV2 = 1024
NFRAG = 8
FRAG = 262144
TOK_REP = 8192
TOKENS = 65536
N_REP = 8


def block_levels(rng, dims, split, smallest, largest):
    def one(dim, blocks):
        heights = jax.random.uniform(jax.random.fold_in(jax.random.fold_in(rng, 6), dim), (blocks,), jnp.float32, smallest / len(split), largest / len(split))
        return jnp.repeat(jnp.exp(heights), dims[dim] // blocks).reshape((-1,) + (1,) * (len(dims) - dim - 1))

    factor_of = one(*split[0])
    for cut in split[1:]:
        factor_of = factor_of * one(*cut)
    return factor_of


def bell_draw(key, extent, spread, limit, cuts=(), held_as=jnp.bfloat16):
    array = jax.random.normal(key, extent, jnp.float32) * spread
    if len(cuts) > 0:
        array = block_levels(key, extent, cuts, -0.22, 0.18) * array
    return jnp.clip(array, min=-limit, max=limit).astype(held_as)


def setup_inputs(seed: int = 0) -> dict:
    splits = jax.random.split(jax.random.key(seed), 8)
    tokens = bell_draw(splits[0], (TOKENS, D), 1.0, 6.0, ((0, 512),))
    kv_weight = bell_draw(splits[1], (N_REP, D, KV2), D ** -0.5, 0.09375, ((0, 8), (1, 64)))
    kv_cotangent = bell_draw(splits[2], (TOKENS, KV2), 1.0, 6.0, ((0, 512),))
    fragment_index = jax.random.randint(splits[3], (1,), 0, NFRAG).astype(jnp.int32)
    anchor = bell_draw(splits[4], (NFRAG, FRAG), 1.0, 6.0, ((1, 64),), jnp.float32)
    momentum = bell_draw(splits[5], (NFRAG, FRAG), 1.0, 6.0, ((1, 64),), jnp.float32)
    replica_frag = bell_draw(splits[6], (N_REP, NFRAG, FRAG), 1.0, 6.0, ((0, 8), (2, 64)))
    return dict(tokens=tokens, kv_weight=kv_weight, kv_cotangent=kv_cotangent, fragment_index=fragment_index, anchor=anchor, momentum=momentum, replica_frag=replica_frag)


norm_eps = 1e-05
outer_momentum = 0.9
outer_rate = 0.7

def reference(tokens, kv_weight, kv_cotangent, fragment_index, anchor, momentum, replica_frag):
    key_parts = []
    input_parts = []
    for replica in range(N_REP):
        rows_in = tokens[replica * TOK_REP:(replica + 1) * TOK_REP].astype(jnp.float32)
        cotan = kv_cotangent[replica * TOK_REP:(replica + 1) * TOK_REP]
        weight = kv_weight[replica]
        inv_rms = lax.rsqrt(lax.optimization_barrier(jnp.mean(rows_in * rows_in, axis=1, keepdims=True)) + norm_eps)
        normed = rows_in * inv_rms
        normed_bf = normed.astype(jnp.bfloat16)
        key_parts.append(jnp.dot(normed_bf, weight, preferred_element_type=jnp.float32).astype(jnp.bfloat16))
        normed_grad = jnp.dot(cotan, weight.T, preferred_element_type=jnp.float32)
        inner = lax.optimization_barrier(jnp.mean(normed_grad * normed, axis=1, keepdims=True))
        input_parts.append((inv_rms * (normed_grad - normed * inner)).astype(jnp.bfloat16))
    frag_pick = fragment_index[0]
    anchor_now = lax.dynamic_index_in_dim(anchor, frag_pick, 0, keepdims=False)
    moment_now = lax.dynamic_index_in_dim(momentum, frag_pick, 0, keepdims=False)
    replica_now = lax.dynamic_index_in_dim(replica_frag, frag_pick, 1, keepdims=False).astype(jnp.float32)
    outer_grad = lax.optimization_barrier(jnp.sum(anchor_now[None, :] - replica_now, axis=0)) / N_REP
    momentum_new = outer_momentum * moment_now + outer_grad
    anchor_new = anchor_now - outer_rate * (outer_grad + outer_momentum * momentum_new)
    return (jnp.concatenate(key_parts, axis=0), jnp.concatenate(input_parts, axis=0), anchor_new, momentum_new)
```

```python
import jax
import jax.numpy as jnp
from jax import lax
from jax.experimental import pallas as pl
from jax.experimental.pallas import tpu as pltpu
from jax.sharding import PartitionSpec as P

norm_eps = 1e-05
outer_momentum = 0.9
outer_rate = 0.7

NY, NZ, NC = 4, 8, 2
FIRST, SECOND = (0, 4, 2, 6), (1, 5, 3, 7)
MIB = 1 << 20


def device_pairs(move):
    pairs = []
    for y in range(NY):
        for z in range(NZ):
            for c in range(NC):
                to_y, to_z, to_c = move(y, z, c)
                pairs.append(((y * NZ + z) * NC + c, ((to_y % NY) * NZ + to_z) * NC + to_c))
    return pairs


def to_z(bit):
    return device_pairs(lambda y, z, c: (y, z ^ bit, c))


def to_y(step):
    return device_pairs(lambda y, z, c: (y + step, z, c))


to_core = device_pairs(lambda y, z, c: (y, z, 1 - c))


def send(x, pairs):
    return lax.ppermute(x, "fsdp", pairs)


def place():
    me = lax.axis_index("fsdp")
    return me // (NZ * NC), lax.rem(me // NC, NZ), lax.rem(me, NC)


def chip_columns(y, z, dy, dz):
    chip = lax.rem(y + (dy + NY), NY) * NZ + jnp.bitwise_xor(z, dz)
    return pl.ds(pl.multiple_of(chip * 128, 128), 128)


def project_kernel(tok_ref, cot_ref, tok_sib_ref, cot_sib_ref, *refs):
    pieces, (out_ref, sib_ref, inv_ref, kv_ref) = refs[:10], refs[10:]
    y, z, c = place()
    rows = tok_ref.shape[0]
    half = lax.broadcasted_iota(jnp.int32, (rows, 128), 1) < 64
    invs = []
    for ref in (tok_ref, tok_sib_ref):
        x = ref[...].astype(jnp.float32)
        invs.append(lax.rsqrt(jnp.mean(x * x, axis=1, keepdims=True) + norm_eps))
    inv_ref[...] = invs[0]
    cot = jnp.concatenate([cot_ref[...], cot_sib_ref[...]], axis=0)
    low = c == 0
    plan = []
    for g in range(2):
        own, left, right, f, s = pieces[5 * g : 5 * g + 5]
        order = (FIRST, SECOND)[g]
        plan += [(0, order, (own,)), (-1, order, (left,)), (1, order, (right,)), (2, order, (f, s))]
    for n, (dy, order, group) in enumerate(plan):
        weight = group[0][...] if len(group) == 1 else jnp.concatenate([group[0][...], group[1][...]], axis=0)
        lhs = []
        for ref, inv in zip((tok_ref, tok_sib_ref), invs):
            cols = []
            for i in (0, 2):
                p = ref[:, chip_columns(y, z, dy, order[i])].astype(jnp.float32) * inv
                q = ref[:, chip_columns(y, z, dy, order[i + 1])].astype(jnp.float32) * inv
                lo = jnp.where(half, p, pltpu.roll(q, 64, 1))
                hi = jnp.where(half, pltpu.roll(p, 64, 1), q)
                cols.append(jnp.where(low, lo, hi).astype(jnp.bfloat16))
            lhs.append(jnp.concatenate(cols, axis=1))
        part = jnp.dot(jnp.concatenate(lhs, axis=0), weight, preferred_element_type=jnp.float32)
        if n == 0:
            kv_ref[...] = part
        else:
            kv_ref[...] += part
        grad = lax.dot_general(cot, weight, (((1,), (1,)), ((), ())), preferred_element_type=jnp.float32)
        out_ref[:, 1024 + 256 * n : 1024 + 256 * (n + 1)] = grad[:rows]
        sib_ref[:, 1024 + 256 * n : 1024 + 256 * (n + 1)] = grad[rows:].astype(jnp.bfloat16)
    out_ref[:, :1024] = kv_ref[:rows]
    sib_ref[:, :1024] = kv_ref[rows:].astype(jnp.bfloat16)


def finish_kernel(tok_ref, inv_ref, own_ref, got_ref, kv_ref, grad_ref, full_ref):
    y, z, c = place()
    rows = tok_ref.shape[0]
    half = lax.broadcasted_iota(jnp.int32, (rows, 128), 1) < 64
    low = c == 0
    inv = inv_ref[...]
    kv_ref[...] = (own_ref[:, :1024] + got_ref[:, :1024].astype(jnp.float32)).astype(jnp.bfloat16)
    total = jnp.zeros((rows, 128), jnp.float32)
    n = 0
    for order in (FIRST, SECOND):
        for dy in (0, -1, 1, 2):
            for i in (0, 2):
                at = 1024 + 256 * n + 64 * i
                mine = own_ref[:, at : at + 128]
                other = got_ref[:, at : at + 128].astype(jnp.float32)
                zero = jnp.where(low, mine, other)
                one = jnp.where(low, other, mine)
                for k, whole in (
                    (0, jnp.where(half, zero, pltpu.roll(one, 64, 1))),
                    (1, jnp.where(half, pltpu.roll(zero, 64, 1), one)),
                ):
                    cols = chip_columns(y, z, dy, order[i + k])
                    full_ref[:, cols] = whole
                    total += whole * (tok_ref[:, cols].astype(jnp.float32) * inv)
            n += 1
    inner = jnp.sum(total, axis=1, keepdims=True) / tok_ref.shape[1]
    normed = tok_ref[...].astype(jnp.float32) * inv
    grad_ref[...] = (inv * (full_ref[...] - normed * inner)).astype(jnp.bfloat16)


def gather_pieces(shard):
    pair = jnp.concatenate([shard, send(shard, to_z(4))], axis=0)
    first = jnp.concatenate([pair, send(pair, to_z(2))], axis=0)
    second = send(first, to_z(1))
    pieces = []
    for own in (first, second):
        h = own.shape[0] // 2
        left = send(own, to_y(1))
        right = send(own, to_y(-1))
        pieces += [own, left, right, send(left[:h], to_y(1)), send(right[h:], to_y(-1))]
    return pieces


def local(tokens, kv_weight, kv_cotangent, fragment_index, anchor, momentum, replica_frag):
    rows, width = tokens.shape
    tok_sib = send(tokens, to_core)
    cot_sib = send(kv_cotangent, to_core)
    pieces = gather_pieces(kv_weight[0])
    params = pltpu.CompilerParams(vmem_limit_bytes=40 * MIB)
    own, for_sib, inv = pl.pallas_call(
        project_kernel,
        out_shape=(
            jax.ShapeDtypeStruct((rows, 1024 + width // 2), jnp.float32),
            jax.ShapeDtypeStruct((rows, 1024 + width // 2), jnp.bfloat16),
            jax.ShapeDtypeStruct((rows, 1), jnp.float32),
        ),
        scratch_shapes=[pltpu.VMEM((2 * rows, 1024), jnp.float32)],
        compiler_params=params,
        cost_estimate=pl.CostEstimate(flops=2**31, bytes_accessed=8 * MIB, transcendentals=256),
        name="project",
    )(tokens, kv_cotangent, tok_sib, cot_sib, *pieces)
    got = send(for_sib, to_core)
    key_value, input_grad = pl.pallas_call(
        finish_kernel,
        out_shape=(
            jax.ShapeDtypeStruct((rows, 1024), jnp.bfloat16),
            jax.ShapeDtypeStruct((rows, width), jnp.bfloat16),
        ),
        scratch_shapes=[pltpu.VMEM((rows, width), jnp.float32)],
        compiler_params=params,
        cost_estimate=pl.CostEstimate(flops=2**22, bytes_accessed=5 * MIB, transcendentals=0),
        name="finish",
    )(tokens, inv, own, got)

    frag_pick = fragment_index[0]
    anchor_now = lax.dynamic_index_in_dim(anchor, frag_pick, 0, keepdims=False)
    moment_now = lax.dynamic_index_in_dim(momentum, frag_pick, 0, keepdims=False)
    replica_now = lax.dynamic_index_in_dim(replica_frag[0], frag_pick, 0, keepdims=False).astype(
        jnp.float32
    )
    replicas = lax.axis_size("rep")
    drift = anchor_now - replica_now
    for bit in (1, 2, 4):
        drift = drift + lax.ppermute(drift, "rep", [(r, r ^ bit) for r in range(replicas)])
    outer_grad = drift / replicas
    momentum_new = outer_momentum * moment_now + outer_grad
    anchor_new = anchor_now - outer_rate * (outer_grad + outer_momentum * momentum_new)
    return key_value, input_grad, anchor_new, momentum_new


def solution(mesh):
    return jax.shard_map(
        local,
        mesh=mesh,
        in_specs=(
            P(("rep", "fsdp"), None),
            P("rep", "fsdp", None),
            P(("rep", "fsdp"), None),
            P(),
            P(None, "fsdp"),
            P(None, "fsdp"),
            P("rep", None, "fsdp"),
        ),
        out_specs=(P(("rep", "fsdp"), None), P(("rep", "fsdp"), None), P("fsdp"), P("fsdp")),
        check_vma=False,
    )
```

```python
import jax
import jax.numpy as jnp
from jax import lax
from jax.experimental import pallas as pl
from jax.experimental.pallas import tpu as pltpu
from jax.sharding import PartitionSpec as P

norm_eps = 1e-05
outer_momentum = 0.9
outer_rate = 0.7

NY, NZ, NC = 4, 8, 2
EVEN = ((0, 4, 2, 6), (0, 2, 4, 6))
ODD = ((1, 5, 3, 7), (1, 3, 5, 7))
WIDE = 1024
MIB = 1 << 20


def device_pairs(move):
    pairs = []
    for y in range(NY):
        for z in range(NZ):
            for c in range(NC):
                to_y, to_z, to_c = move(y, z, c)
                pairs.append(((y * NZ + z) * NC + c, ((to_y % NY) * NZ + to_z) * NC + to_c))
    return pairs


def to_z(*bits):
    return device_pairs(lambda y, z, c: (y, z ^ bits[c], c))


def to_y(step):
    return device_pairs(lambda y, z, c: (y + step, z, c))


to_core = device_pairs(lambda y, z, c: (y, z, 1 - c))


def send(x, pairs):
    return lax.ppermute(x, "fsdp", pairs)


def place():
    me = lax.axis_index("fsdp")
    return me // (NZ * NC), lax.rem(me // NC, NZ), lax.rem(me, NC)


def slab(y, step):
    return pl.ds(pl.multiple_of(lax.rem(y + step, NY) * WIDE, WIDE), WIDE)


def prepare_kernel(tok_ref, cot_ref, *refs):
    outs, inv_ref = refs[:NY], refs[NY]
    y, _, _ = place()
    x = tok_ref[...].astype(jnp.float32)
    inv = lax.rsqrt(jnp.mean(x * x, axis=1, keepdims=True) + norm_eps)
    inv_ref[...] = inv
    for step, out_ref in enumerate(outs):
        out_ref[:, :WIDE] = (tok_ref[:, slab(y, step)].astype(jnp.float32) * inv).astype(jnp.bfloat16)
        out_ref[:, WIDE:] = cot_ref[...]


def project_kernel(first_ref, second_ref, first_sib_ref, second_sib_ref, *refs):
    ins, (own_ref, *outs), (weight_ref, act_ref) = refs[:NY], refs[NY : 2 * NY], refs[2 * NY :]
    _, z, c = place()
    rows = ins[0].shape[0]
    for sib, pair in enumerate(((first_ref, second_ref), (first_sib_ref, second_sib_ref))):
        core = lax.rem(c + sib, NC)
        for order, ref in zip((EVEN, ODD), pair):
            for i in range(4):
                dz = jnp.where(core == 0, order[0][i], order[1][i])
                at = pl.multiple_of(jnp.bitwise_xor(z, dz) * 128 + core * 64, 64)
                weight_ref[pl.ds(at, 64)] = ref[64 * i : 64 * (i + 1)]
    for n, ref in enumerate(ins):
        act_ref[rows * n : rows * (n + 1)] = ref[...]
    for half in range(2):
        for i in range(WIDE // 256):
            cols = slice(256 * i, 256 * (i + 1))
            if half == 0:
                part = jnp.dot(act_ref[:, :WIDE], weight_ref[:, cols], preferred_element_type=jnp.float32)
            else:
                part = lax.dot_general(
                    act_ref[:, WIDE:],
                    weight_ref[cols],
                    (((1,), (1,)), ((), ())),
                    preferred_element_type=jnp.float32,
                )
            cols = slice(WIDE * half + 256 * i, WIDE * half + 256 * (i + 1))
            own_ref[:, cols] = part[:rows]
            for n, out_ref in enumerate(outs, 1):
                out_ref[:, cols] = part[rows * n : rows * (n + 1)].astype(jnp.bfloat16)


def finish_kernel(tok_ref, inv_ref, own_ref, *refs):
    gots, (kv_ref, grad_ref, full_ref) = refs[: NY - 1], refs[NY - 1 :]
    y, _, _ = place()
    inv = inv_ref[...]
    kv = own_ref[:, :WIDE]
    for ref in gots:
        kv += ref[:, :WIDE].astype(jnp.float32)
    kv_ref[...] = kv.astype(jnp.bfloat16)
    inner = 0.0
    for step, ref in enumerate((own_ref, *gots)):
        cols = slab(y, step)
        grad = ref[:, WIDE:].astype(jnp.float32)
        full_ref[:, cols] = grad
        inner += jnp.sum(grad * (tok_ref[:, cols].astype(jnp.float32) * inv), axis=1, keepdims=True)
    inner = inner / tok_ref.shape[1]
    normed = tok_ref[...].astype(jnp.float32) * inv
    grad_ref[...] = (inv * (full_ref[...] - normed * inner)).astype(jnp.bfloat16)


def local(tokens, kv_weight, kv_cotangent, fragment_index, anchor, momentum, replica_frag):
    rows, width = tokens.shape
    shard = kv_weight[0]
    tie = lax.optimization_barrier
    params = pltpu.CompilerParams(vmem_limit_bytes=40 * MIB)

    frag_pick = fragment_index[0]
    anchor_now = lax.dynamic_index_in_dim(anchor, frag_pick, 0, keepdims=False)
    moment_now = lax.dynamic_index_in_dim(momentum, frag_pick, 0, keepdims=False)
    replica_now = lax.dynamic_index_in_dim(replica_frag[0], frag_pick, 0, keepdims=False).astype(
        jnp.float32
    )
    replicas = lax.axis_size("rep")
    drift = anchor_now - replica_now

    def add_half(drift, bit):
        return drift + lax.ppermute(drift, "rep", [(r, r ^ bit) for r in range(replicas)])

    block = jax.ShapeDtypeStruct((rows, 2 * WIDE), jnp.bfloat16)
    *acts, inv = pl.pallas_call(
        prepare_kernel,
        out_shape=(block,) * NY + (jax.ShapeDtypeStruct((rows, 1), jnp.float32),),
        compiler_params=params,
        cost_estimate=pl.CostEstimate(flops=2**21, bytes_accessed=4 * MIB, transcendentals=128),
        name="prepare",
    )(tokens, kv_cotangent)

    far = send(shard, to_z(4, 2))
    act1 = send(acts[1], to_y(1))
    act3 = send(acts[3], to_y(3))
    far, drift = tie((far, drift))
    pair = jnp.concatenate([shard, far], axis=0)
    more = send(pair, to_z(2, 4))
    pair, drift = tie((pair, drift))
    drift = add_half(drift, 2)
    drift, acts[2] = tie((drift, acts[2]))
    act2 = send(acts[2], to_y(2))
    more, drift, act1 = tie((more, drift, act1))
    first = jnp.concatenate([pair, more], axis=0)
    second = send(first, to_z(1, 1))
    first_sib = send(first, to_core)
    drift = add_half(drift, 4)
    second, act2, act3, drift = tie((second, act2, act3, drift))
    acts = [acts[0], act1, act2, act3]
    second_sib = send(second, to_core)
    weights = (first, second, first_sib, second_sib)
    own, *backs = pl.pallas_call(
        project_kernel,
        out_shape=(jax.ShapeDtypeStruct((rows, 2 * WIDE), jnp.float32),) + (block,) * (NY - 1),
        scratch_shapes=[
            pltpu.VMEM((WIDE, WIDE), jnp.bfloat16),
            pltpu.VMEM((NY * rows, 2 * WIDE), jnp.bfloat16),
        ],
        compiler_params=params,
        cost_estimate=pl.CostEstimate(flops=2**31, bytes_accessed=8 * MIB, transcendentals=0),
        name="project",
    )(*weights, *acts)
    drift, *backs = tie((drift, *backs))
    gots = [send(backs[n - 1], to_y(-n)) for n in (1, 3, 2)]
    gots = [gots[0], gots[2], gots[1]]
    drift = add_half(drift, 1)
    outer_grad = drift / replicas
    momentum_new = outer_momentum * moment_now + outer_grad
    anchor_new = anchor_now - outer_rate * (outer_grad + outer_momentum * momentum_new)
    key_value, input_grad = pl.pallas_call(
        finish_kernel,
        out_shape=(
            jax.ShapeDtypeStruct((rows, WIDE), jnp.bfloat16),
            jax.ShapeDtypeStruct((rows, width), jnp.bfloat16),
        ),
        scratch_shapes=[pltpu.VMEM((rows, width), jnp.float32)],
        compiler_params=params,
        cost_estimate=pl.CostEstimate(flops=2**22, bytes_accessed=5 * MIB, transcendentals=0),
        name="finish",
    )(tokens, inv, own, *gots)
    return key_value, input_grad, anchor_new, momentum_new


def solution(mesh):
    return jax.shard_map(
        local,
        mesh=mesh,
        in_specs=(
            P(("rep", "fsdp"), None),
            P("rep", "fsdp", None),
            P(("rep", "fsdp"), None),
            P(),
            P(None, "fsdp"),
            P(None, "fsdp"),
            P("rep", None, "fsdp"),
        ),
        out_specs=(P(("rep", "fsdp"), None), P(("rep", "fsdp"), None), P("fsdp"), P("fsdp")),
        check_vma=False,
    )
```

```python
import jax
import jax.numpy as jnp
from jax import lax
from jax.experimental import pallas as pl
from jax.experimental.pallas import tpu as pltpu
from jax.sharding import PartitionSpec as P

norm_eps = 1e-05
outer_momentum = 0.9
outer_rate = 0.7

NY, NZ, NC = 4, 8, 2
EVEN = ((0, 4, 2, 6), (0, 2, 4, 6))
ODD = ((1, 5, 3, 7), (1, 3, 5, 7))
WIDE = 1024
MIB = 1 << 20


def device_pairs(move):
    pairs = []
    for y in range(NY):
        for z in range(NZ):
            for c in range(NC):
                to_y, to_z, to_c = move(y, z, c)
                pairs.append(((y * NZ + z) * NC + c, ((to_y % NY) * NZ + to_z) * NC + to_c))
    return pairs


def to_z(*bits):
    return device_pairs(lambda y, z, c: (y, z ^ bits[c], c))


def to_y(step):
    return device_pairs(lambda y, z, c: (y + step, z, c))


to_core = device_pairs(lambda y, z, c: (y, z, 1 - c))


def send(x, pairs):
    return lax.ppermute(x, "fsdp", pairs)


def place():
    me = lax.axis_index("fsdp")
    return me // (NZ * NC), lax.rem(me // NC, NZ), lax.rem(me, NC)


def slab(y, step):
    return pl.ds(pl.multiple_of(lax.rem(y + step, NY) * WIDE, WIDE), WIDE)


def prepare_kernel(tok_ref, cot_ref, *refs):
    outs, inv_ref = refs[:NY], refs[NY]
    y, _, _ = place()
    x = tok_ref[...].astype(jnp.float32)
    inv = lax.rsqrt(jnp.mean(x * x, axis=1, keepdims=True) + norm_eps)
    inv_ref[...] = inv
    for step, out_ref in enumerate(outs):
        out_ref[:, :WIDE] = (tok_ref[:, slab(y, step)].astype(jnp.float32) * inv).astype(jnp.bfloat16)
        out_ref[:, WIDE:] = cot_ref[...]


def project_kernel(first_ref, second_ref, first_sib_ref, second_sib_ref, *refs):
    ins, (own_ref, *outs), (weight_ref, act_ref) = refs[:NY], refs[NY : 2 * NY], refs[2 * NY :]
    _, z, c = place()
    rows = ins[0].shape[0]
    for sib, pair in enumerate(((first_ref, second_ref), (first_sib_ref, second_sib_ref))):
        core = lax.rem(c + sib, NC)
        for order, ref in zip((EVEN, ODD), pair):
            for i in range(4):
                dz = jnp.where(core == 0, order[0][i], order[1][i])
                at = pl.multiple_of(jnp.bitwise_xor(z, dz) * 128 + core * 64, 64)
                weight_ref[pl.ds(at, 64)] = ref[64 * i : 64 * (i + 1)]
    for n, ref in enumerate(ins):
        act_ref[rows * n : rows * (n + 1)] = ref[...]
    for half in range(2):
        for i in range(WIDE // 256):
            cols = slice(256 * i, 256 * (i + 1))
            if half == 0:
                part = jnp.dot(act_ref[:, :WIDE], weight_ref[:, cols], preferred_element_type=jnp.float32)
            else:
                part = lax.dot_general(
                    act_ref[:, WIDE:],
                    weight_ref[cols],
                    (((1,), (1,)), ((), ())),
                    preferred_element_type=jnp.float32,
                )
            cols = slice(WIDE * half + 256 * i, WIDE * half + 256 * (i + 1))
            own_ref[:, cols] = part[:rows]
            for n, out_ref in enumerate(outs, 1):
                out_ref[:, cols] = part[rows * n : rows * (n + 1)].astype(jnp.bfloat16)


def finish_kernel(tok_ref, inv_ref, own_ref, *refs):
    gots, (kv_ref, grad_ref, full_ref) = refs[: NY - 1], refs[NY - 1 :]
    y, _, _ = place()
    inv = inv_ref[...]
    kv = own_ref[:, :WIDE]
    for ref in gots:
        kv += ref[:, :WIDE].astype(jnp.float32)
    kv_ref[...] = kv.astype(jnp.bfloat16)
    inner = 0.0
    for step, ref in zip((0, 2, 1, 3), (own_ref, *gots)):
        cols = slab(y, step)
        grad = ref[:, WIDE:].astype(jnp.float32)
        full_ref[:, cols] = grad
        inner += jnp.sum(grad * (tok_ref[:, cols].astype(jnp.float32) * inv), axis=1, keepdims=True)
    inner = inner / tok_ref.shape[1]
    normed = tok_ref[...].astype(jnp.float32) * inv
    grad_ref[...] = (inv * (full_ref[...] - normed * inner)).astype(jnp.bfloat16)


def local(tokens, kv_weight, kv_cotangent, fragment_index, anchor, momentum, replica_frag):
    rows, width = tokens.shape
    shard = kv_weight[0]
    tie = lax.optimization_barrier
    params = pltpu.CompilerParams(vmem_limit_bytes=40 * MIB)

    frag_pick = fragment_index[0]
    anchor_now = lax.dynamic_index_in_dim(anchor, frag_pick, 0, keepdims=False)
    moment_now = lax.dynamic_index_in_dim(momentum, frag_pick, 0, keepdims=False)
    replica_now = lax.dynamic_index_in_dim(replica_frag[0], frag_pick, 0, keepdims=False).astype(
        jnp.float32
    )
    replicas = lax.axis_size("rep")
    drift = anchor_now - replica_now

    def add_half(drift, bit):
        return drift + lax.ppermute(drift, "rep", [(r, r ^ bit) for r in range(replicas)])

    block = jax.ShapeDtypeStruct((rows, 2 * WIDE), jnp.bfloat16)
    *acts, inv = pl.pallas_call(
        prepare_kernel,
        out_shape=(block,) * NY + (jax.ShapeDtypeStruct((rows, 1), jnp.float32),),
        compiler_params=params,
        cost_estimate=pl.CostEstimate(flops=2**21, bytes_accessed=4 * MIB, transcendentals=128),
        name="prepare",
    )(tokens, kv_cotangent)

    far = send(shard, to_z(4, 2))
    act1 = send(acts[1], to_y(1))
    act3 = send(acts[3], to_y(3))
    far, drift = tie((far, drift))
    pair = jnp.concatenate([shard, far], axis=0)
    more = send(pair, to_z(2, 4))
    pair, drift = tie((pair, drift))
    drift = add_half(drift, 2)
    drift, acts[2] = tie((drift, acts[2]))
    act2 = send(acts[2], to_y(2))
    more, drift, act1 = tie((more, drift, act1))
    first = jnp.concatenate([pair, more], axis=0)
    second = send(first, to_z(1, 1))
    first_sib = send(first, to_core)
    drift = add_half(drift, 4)
    second, act2, act3, drift = tie((second, act2, act3, drift))
    acts = [acts[0], act1, act2, act3]
    second_sib = send(second, to_core)
    weights = (first, second, first_sib, second_sib)
    own, *backs = pl.pallas_call(
        project_kernel,
        out_shape=(jax.ShapeDtypeStruct((rows, 2 * WIDE), jnp.float32),) + (block,) * (NY - 1),
        scratch_shapes=[
            pltpu.VMEM((WIDE, WIDE), jnp.bfloat16),
            pltpu.VMEM((NY * rows, 2 * WIDE), jnp.bfloat16),
        ],
        compiler_params=params,
        cost_estimate=pl.CostEstimate(flops=2**31, bytes_accessed=8 * MIB, transcendentals=0),
        name="project",
    )(*weights, *acts)
    drift, *backs = tie((drift, *backs))
    gots = [send(backs[n - 1], to_y(-n)) for n in (2, 1, 3)]
    drift = add_half(drift, 1)
    outer_grad = drift / replicas
    momentum_new = outer_momentum * moment_now + outer_grad
    anchor_new = anchor_now - outer_rate * (outer_grad + outer_momentum * momentum_new)
    key_value, input_grad = pl.pallas_call(
        finish_kernel,
        out_shape=(
            jax.ShapeDtypeStruct((rows, WIDE), jnp.bfloat16),
            jax.ShapeDtypeStruct((rows, width), jnp.bfloat16),
        ),
        scratch_shapes=[pltpu.VMEM((rows, width), jnp.float32)],
        compiler_params=params,
        cost_estimate=pl.CostEstimate(flops=2**22, bytes_accessed=5 * MIB, transcendentals=0),
        name="finish",
    )(tokens, inv, own, *gots)
    return key_value, input_grad, anchor_new, momentum_new


def solution(mesh):
    return jax.shard_map(
        local,
        mesh=mesh,
        in_specs=(
            P(("rep", "fsdp"), None),
            P("rep", "fsdp", None),
            P(("rep", "fsdp"), None),
            P(),
            P(None, "fsdp"),
            P(None, "fsdp"),
            P("rep", None, "fsdp"),
        ),
        out_specs=(P(("rep", "fsdp"), None), P(("rep", "fsdp"), None), P("fsdp"), P("fsdp")),
        check_vma=False,
    )
```

```python
import jax
import jax.numpy as jnp
from jax import lax
from jax.experimental import pallas as pl
from jax.experimental.pallas import tpu as pltpu
from jax.sharding import PartitionSpec as P

norm_eps = 1e-05
outer_momentum = 0.9
outer_rate = 0.7

NY, NZ, NC = 4, 8, 2
EVEN = ((0, 4, 2, 6), (0, 2, 4, 6))
ODD = ((1, 5, 3, 7), (1, 3, 5, 7))
WIDE = 1024
HALF = WIDE // 2
MIB = 1 << 20


def device_pairs(move):
    pairs = []
    for y in range(NY):
        for z in range(NZ):
            for c in range(NC):
                to_y, to_z, to_c = move(y, z, c)
                pairs.append(((y * NZ + z) * NC + c, ((to_y % NY) * NZ + to_z) * NC + to_c))
    return pairs


def to_z(*bits):
    return device_pairs(lambda y, z, c: (y, z ^ bits[c], c))


def to_y(step):
    return device_pairs(lambda y, z, c: (y + step, z, c))


to_core = device_pairs(lambda y, z, c: (y, z, 1 - c))


def send(x, pairs):
    return lax.ppermute(x, "fsdp", pairs)


def place():
    me = lax.axis_index("fsdp")
    return me // (NZ * NC), lax.rem(me // NC, NZ), lax.rem(me, NC)


def slab(y, step):
    return pl.ds(pl.multiple_of(lax.rem(y + step, NY) * WIDE, WIDE), WIDE)


def prepare_kernel(tok_ref, cot_ref, *refs):
    outs, inv_ref = refs[:NY], refs[NY]
    y, _, _ = place()
    x = tok_ref[...].astype(jnp.float32)
    inv = lax.rsqrt(jnp.mean(x * x, axis=1, keepdims=True) + norm_eps)
    inv_ref[...] = inv
    for step, out_ref in enumerate(outs):
        out_ref[:, :WIDE] = (tok_ref[:, slab(y, step)].astype(jnp.float32) * inv).astype(jnp.bfloat16)
        out_ref[:, WIDE:] = cot_ref[...]


def half_of_features(mine_ref, sib_ref, order, acts, weight_ref, lhs_ref):
    _, z, c = place()
    rows = acts[0].shape[0]
    for sib, ref in enumerate((mine_ref, sib_ref)):
        core = lax.rem(c + sib, NC)
        for i in range(4):
            chip = jnp.bitwise_xor(z, jnp.where(core == 0, order[0][i], order[1][i]))
            at = pl.multiple_of(chip // 2 * 128 + core * 64, 64)
            weight_ref[pl.ds(at, 64)] = ref[64 * i : 64 * (i + 1)]
    odd = lax.rem(z + order[0][0], 2)
    for n, ref in enumerate(acts):
        lhs_ref[rows * n : rows * (n + 1), HALF:] = ref[:, WIDE:]
        for i in range(4):
            cols = pl.ds(pl.multiple_of((2 * i + odd) * 128, 128), 128)
            lhs_ref[rows * n : rows * (n + 1), 128 * i : 128 * (i + 1)] = ref[:, cols]


def first_kernel(mine_ref, sib_ref, *refs):
    acts, (kv_ref, own_ref, *outs), (weight_ref, lhs_ref) = refs[:NY], refs[NY:-2], refs[-2:]
    rows = acts[0].shape[0]
    half_of_features(mine_ref, sib_ref, EVEN, acts, weight_ref, lhs_ref)
    for i in range(HALF // 256):
        cols = slice(256 * i, 256 * (i + 1))
        part = lax.dot_general(
            lhs_ref[:, HALF:], weight_ref[cols], (((1,), (1,)), ((), ())), preferred_element_type=jnp.float32
        )
        own_ref[:, cols] = part[:rows]
        for n, out_ref in enumerate(outs, 1):
            out_ref[:, cols] = part[rows * n : rows * (n + 1)].astype(jnp.bfloat16)
    for i in range(WIDE // 256):
        cols = slice(256 * i, 256 * (i + 1))
        kv_ref[:, cols] = jnp.dot(lhs_ref[:, :HALF], weight_ref[:, cols], preferred_element_type=jnp.float32)


def second_kernel(mine_ref, sib_ref, kv_ref, *refs):
    acts, firsts, (own_ref, *outs), (weight_ref, lhs_ref) = (
        refs[:NY], refs[NY : 2 * NY], refs[2 * NY : -2], refs[-2:]
    )
    _, z, _ = place()
    rows = acts[0].shape[0]
    half_of_features(mine_ref, sib_ref, ODD, acts, weight_ref, lhs_ref)
    for i in range(WIDE // 256):
        cols = slice(256 * i, 256 * (i + 1))
        part = kv_ref[:, cols] + jnp.dot(
            lhs_ref[:, :HALF], weight_ref[:, cols], preferred_element_type=jnp.float32
        )
        own_ref[:, cols] = part[:rows]
        for n, out_ref in enumerate(outs, 1):
            out_ref[:, cols] = part[rows * n : rows * (n + 1)].astype(jnp.bfloat16)
    even, odd = lax.rem(z, 2), lax.rem(z + 1, 2)
    for i in range(HALF // 128):
        cols = pl.ds(pl.multiple_of(WIDE + (2 * i + even) * 128, 128), 128)
        for out_ref, first_ref in zip((own_ref, *outs), firsts):
            out_ref[:, cols] = first_ref[:, 128 * i : 128 * (i + 1)]
    for i in range(HALF // 256):
        part = lax.dot_general(
            lhs_ref[:, HALF:],
            weight_ref[256 * i : 256 * (i + 1)],
            (((1,), (1,)), ((), ())),
            preferred_element_type=jnp.float32,
        )
        for k in range(2):
            cols = pl.ds(pl.multiple_of(WIDE + (4 * i + 2 * k + odd) * 128, 128), 128)
            turn = part[:, 128 * k : 128 * (k + 1)]
            own_ref[:, cols] = turn[:rows]
            for n, out_ref in enumerate(outs, 1):
                out_ref[:, cols] = turn[rows * n : rows * (n + 1)].astype(jnp.bfloat16)


def finish_kernel(tok_ref, inv_ref, own_ref, *refs):
    gots, (kv_ref, grad_ref) = refs[: NY - 1], refs[NY - 1 :]
    y, _, _ = place()
    inv = inv_ref[...]
    kv = own_ref[:, :WIDE]
    for ref in gots:
        kv += ref[:, :WIDE].astype(jnp.float32)
    kv_ref[...] = kv.astype(jnp.bfloat16)
    sources = list(zip((0, 2, 1, 3), (own_ref, *gots)))
    inner = 0.0
    for step, ref in sources:
        normed = tok_ref[:, slab(y, step)].astype(jnp.float32) * inv
        inner += jnp.sum(ref[:, WIDE:].astype(jnp.float32) * normed, axis=1, keepdims=True)
    inner = inner / tok_ref.shape[1]
    for step, ref in sources:
        normed = tok_ref[:, slab(y, step)].astype(jnp.float32) * inv
        grad = ref[:, WIDE:].astype(jnp.float32)
        grad_ref[:, slab(y, step)] = (inv * (grad - normed * inner)).astype(jnp.bfloat16)


def local(tokens, kv_weight, kv_cotangent, fragment_index, anchor, momentum, replica_frag):
    rows, width = tokens.shape
    shard = kv_weight[0]
    tie = lax.optimization_barrier
    params = pltpu.CompilerParams(vmem_limit_bytes=24 * MIB)

    frag_pick = fragment_index[0]
    anchor_now = lax.dynamic_index_in_dim(anchor, frag_pick, 0, keepdims=False)
    moment_now = lax.dynamic_index_in_dim(momentum, frag_pick, 0, keepdims=False)
    replica_now = lax.dynamic_index_in_dim(replica_frag[0], frag_pick, 0, keepdims=False).astype(
        jnp.float32
    )
    replicas = lax.axis_size("rep")
    drift = anchor_now - replica_now

    def add_half(drift, bit):
        return drift + lax.ppermute(drift, "rep", [(r, r ^ bit) for r in range(replicas)])

    block = jax.ShapeDtypeStruct((rows, 2 * WIDE), jnp.bfloat16)
    *acts, inv = pl.pallas_call(
        prepare_kernel,
        out_shape=(block,) * NY + (jax.ShapeDtypeStruct((rows, 1), jnp.float32),),
        compiler_params=params,
        cost_estimate=pl.CostEstimate(flops=2**21, bytes_accessed=4 * MIB, transcendentals=128),
        name="prepare",
    )(tokens, kv_cotangent)

    far = send(shard, to_z(4, 2))
    act1 = send(acts[1], to_y(1))
    act3 = send(acts[3], to_y(3))
    far, drift = tie((far, drift))
    pair = jnp.concatenate([shard, far], axis=0)
    more = send(pair, to_z(2, 4))
    pair, drift = tie((pair, drift))
    drift = add_half(drift, 2)
    drift, acts[2] = tie((drift, acts[2]))
    act2 = send(acts[2], to_y(2))
    more, drift, act1 = tie((more, drift, act1))
    first = jnp.concatenate([pair, more], axis=0)
    second = send(first, to_z(1, 1))
    first_sib = send(first, to_core)
    drift = add_half(drift, 4)
    second, first_sib, act2, act3, drift = tie((second, first_sib, act2, act3, drift))
    acts = [acts[0], act1, act2, act3]
    second_sib = send(second, to_core)
    scratch = [pltpu.VMEM((HALF, WIDE), jnp.bfloat16), pltpu.VMEM((NY * rows, HALF + WIDE), jnp.bfloat16)]
    kv_first, own_first, *grads_first = pl.pallas_call(
        first_kernel,
        out_shape=(
            jax.ShapeDtypeStruct((NY * rows, WIDE), jnp.float32),
            jax.ShapeDtypeStruct((rows, HALF), jnp.float32),
        )
        + (jax.ShapeDtypeStruct((rows, HALF), jnp.bfloat16),) * (NY - 1),
        scratch_shapes=scratch,
        compiler_params=params,
        cost_estimate=pl.CostEstimate(flops=2**30, bytes_accessed=8 * MIB, transcendentals=0),
        name="first_half",
    )(first, first_sib, *acts)
    own, *backs = pl.pallas_call(
        second_kernel,
        out_shape=(jax.ShapeDtypeStruct((rows, 2 * WIDE), jnp.float32),) + (block,) * (NY - 1),
        scratch_shapes=scratch,
        compiler_params=params,
        cost_estimate=pl.CostEstimate(flops=2**30, bytes_accessed=8 * MIB, transcendentals=0),
        name="second_half",
    )(second, second_sib, kv_first, *acts, own_first, *grads_first)
    drift, *backs = tie((drift, *backs))
    gots = [send(backs[n - 1], to_y(-n)) for n in (2, 1, 3)]
    drift = add_half(drift, 1)
    outer_grad = drift / replicas
    momentum_new = outer_momentum * moment_now + outer_grad
    anchor_new = anchor_now - outer_rate * (outer_grad + outer_momentum * momentum_new)
    key_value, input_grad = pl.pallas_call(
        finish_kernel,
        out_shape=(
            jax.ShapeDtypeStruct((rows, WIDE), jnp.bfloat16),
            jax.ShapeDtypeStruct((rows, width), jnp.bfloat16),
        ),
        compiler_params=params,
        cost_estimate=pl.CostEstimate(flops=2**22, bytes_accessed=5 * MIB, transcendentals=0),
        name="finish",
    )(tokens, inv, own, *gots)
    return key_value, input_grad, anchor_new, momentum_new


def solution(mesh):
    return jax.shard_map(
        local,
        mesh=mesh,
        in_specs=(
            P(("rep", "fsdp"), None),
            P("rep", "fsdp", None),
            P(("rep", "fsdp"), None),
            P(),
            P(None, "fsdp"),
            P(None, "fsdp"),
            P("rep", None, "fsdp"),
        ),
        out_specs=(P(("rep", "fsdp"), None), P(("rep", "fsdp"), None), P("fsdp"), P("fsdp")),
        check_vma=False,
    )
```

```python
import jax
import jax.numpy as jnp
from jax import lax
from jax.experimental import pallas as pl
from jax.experimental.pallas import tpu as pltpu
from jax.sharding import PartitionSpec as P

norm_eps = 1e-05
outer_momentum = 0.9
outer_rate = 0.7

NY, NZ, NC = 4, 8, 2
EVEN = ((0, 2, 4, 6), (0, 4, 2, 6))
ODD = ((1, 3, 5, 7), (1, 5, 3, 7))
WIDE = 1024
HALF = WIDE // 2
MIB = 1 << 20


def device_pairs(move):
    pairs = []
    for y in range(NY):
        for z in range(NZ):
            for c in range(NC):
                to_y, to_z, to_c = move(y, z, c)
                pairs.append(((y * NZ + z) * NC + c, ((to_y % NY) * NZ + to_z) * NC + to_c))
    return pairs


def to_z(*bits):
    return device_pairs(lambda y, z, c: (y, z ^ bits[c], c))


def to_y(step):
    return device_pairs(lambda y, z, c: (y + step, z, c))


to_core = device_pairs(lambda y, z, c: (y, z, 1 - c))


def send(x, pairs):
    return lax.ppermute(x, "fsdp", pairs)


def place():
    me = lax.axis_index("fsdp")
    return me // (NZ * NC), lax.rem(me // NC, NZ), lax.rem(me, NC)


def slab(y, step):
    return pl.ds(pl.multiple_of(lax.rem(y + step, NY) * WIDE, WIDE), WIDE)


def prepare_kernel(tok_ref, cot_ref, shard_ref, *refs):
    outs, inv_ref, kept_ref = refs[:NY], refs[NY], refs[NY + 1]
    y, _, _ = place()
    kept_ref[...] = shard_ref[...]
    x = tok_ref[...].astype(jnp.float32)
    inv = lax.rsqrt(jnp.mean(x * x, axis=1, keepdims=True) + norm_eps)
    inv_ref[...] = inv
    for step, out_ref in enumerate(outs):
        out_ref[:, :WIDE] = (tok_ref[:, slab(y, step)].astype(jnp.float32) * inv).astype(jnp.bfloat16)
        out_ref[:, WIDE:] = cot_ref[...]


def half_of_features(mine_ref, sib_ref, order, acts, weight_ref, lhs_ref):
    _, z, c = place()
    rows = acts[0].shape[0]
    for sib, ref in enumerate((mine_ref, sib_ref)):
        core = lax.rem(c + sib, NC)
        for i in range(4):
            chip = jnp.bitwise_xor(z, jnp.where(core == 0, order[0][i], order[1][i]))
            at = pl.multiple_of(chip // 2 * 128 + core * 64, 64)
            weight_ref[pl.ds(at, 64)] = ref[64 * i : 64 * (i + 1)]
    odd = lax.rem(z + order[0][0], 2)
    for n, ref in enumerate(acts):
        lhs_ref[rows * n : rows * (n + 1), HALF:] = ref[:, WIDE:]
        for i in range(4):
            cols = pl.ds(pl.multiple_of((2 * i + odd) * 128, 128), 128)
            lhs_ref[rows * n : rows * (n + 1), 128 * i : 128 * (i + 1)] = ref[:, cols]


def first_kernel(mine_ref, sib_ref, *refs):
    acts, (kv_ref, own_ref, *outs), (weight_ref, lhs_ref) = refs[:NY], refs[NY:-2], refs[-2:]
    rows = acts[0].shape[0]
    half_of_features(mine_ref, sib_ref, EVEN, acts, weight_ref, lhs_ref)
    for i in range(HALF // 256):
        cols = slice(256 * i, 256 * (i + 1))
        part = lax.dot_general(
            lhs_ref[:, HALF:], weight_ref[cols], (((1,), (1,)), ((), ())), preferred_element_type=jnp.float32
        )
        own_ref[:, cols] = part[:rows]
        for n, out_ref in enumerate(outs, 1):
            out_ref[:, cols] = part[rows * n : rows * (n + 1)].astype(jnp.bfloat16)
    for i in range(WIDE // 256):
        cols = slice(256 * i, 256 * (i + 1))
        kv_ref[:, cols] = jnp.dot(lhs_ref[:, :HALF], weight_ref[:, cols], preferred_element_type=jnp.float32)


def second_kernel(mine_ref, sib_ref, kv_ref, *refs):
    acts, firsts, (own_ref, *outs), (weight_ref, lhs_ref) = (
        refs[:NY], refs[NY : 2 * NY], refs[2 * NY : -2], refs[-2:]
    )
    _, z, _ = place()
    rows = acts[0].shape[0]
    half_of_features(mine_ref, sib_ref, ODD, acts, weight_ref, lhs_ref)
    for i in range(WIDE // 256):
        cols = slice(256 * i, 256 * (i + 1))
        part = kv_ref[:, cols] + jnp.dot(
            lhs_ref[:, :HALF], weight_ref[:, cols], preferred_element_type=jnp.float32
        )
        own_ref[:, cols] = part[:rows]
        for n, out_ref in enumerate(outs, 1):
            out_ref[:, cols] = part[rows * n : rows * (n + 1)].astype(jnp.bfloat16)
    even, odd = lax.rem(z, 2), lax.rem(z + 1, 2)
    for i in range(HALF // 128):
        cols = pl.ds(pl.multiple_of(WIDE + (2 * i + even) * 128, 128), 128)
        for out_ref, first_ref in zip((own_ref, *outs), firsts):
            out_ref[:, cols] = first_ref[:, 128 * i : 128 * (i + 1)]
    for i in range(HALF // 256):
        part = lax.dot_general(
            lhs_ref[:, HALF:],
            weight_ref[256 * i : 256 * (i + 1)],
            (((1,), (1,)), ((), ())),
            preferred_element_type=jnp.float32,
        )
        for k in range(2):
            cols = pl.ds(pl.multiple_of(WIDE + (4 * i + 2 * k + odd) * 128, 128), 128)
            turn = part[:, 128 * k : 128 * (k + 1)]
            own_ref[:, cols] = turn[:rows]
            for n, out_ref in enumerate(outs, 1):
                out_ref[:, cols] = turn[rows * n : rows * (n + 1)].astype(jnp.bfloat16)


def begin_kernel(tok_ref, inv_ref, own_ref, across_ref, kv_ref, inner_ref):
    y, _, _ = place()
    inv = inv_ref[...]
    kv_ref[...] = own_ref[:, :WIDE] + across_ref[:, :WIDE].astype(jnp.float32)
    inner = 0.0
    for step, ref in ((0, own_ref), (2, across_ref)):
        normed = tok_ref[:, slab(y, step)].astype(jnp.float32) * inv
        inner += jnp.sum(ref[:, WIDE:].astype(jnp.float32) * normed, axis=1, keepdims=True)
    inner_ref[...] = inner


def finish_kernel(tok_ref, inv_ref, kv_part_ref, inner_ref, own_ref, *refs):
    gots, (kv_ref, grad_ref) = refs[: NY - 1], refs[NY - 1 :]
    y, _, _ = place()
    inv = inv_ref[...]
    kv = kv_part_ref[...]
    for ref in gots[1:]:
        kv += ref[:, :WIDE].astype(jnp.float32)
    kv_ref[...] = kv.astype(jnp.bfloat16)
    sources = list(zip((0, 2, 1, 3), (own_ref, *gots)))
    inner = inner_ref[...]
    for step, ref in sources[2:]:
        normed = tok_ref[:, slab(y, step)].astype(jnp.float32) * inv
        inner += jnp.sum(ref[:, WIDE:].astype(jnp.float32) * normed, axis=1, keepdims=True)
    inner = inner / tok_ref.shape[1]
    for step, ref in sources:
        normed = tok_ref[:, slab(y, step)].astype(jnp.float32) * inv
        grad = ref[:, WIDE:].astype(jnp.float32)
        grad_ref[:, slab(y, step)] = (inv * (grad - normed * inner)).astype(jnp.bfloat16)


def local(tokens, kv_weight, kv_cotangent, fragment_index, anchor, momentum, replica_frag):
    rows, width = tokens.shape
    shard = kv_weight[0]
    tie = lax.optimization_barrier
    params = pltpu.CompilerParams(vmem_limit_bytes=24 * MIB)

    frag_pick = fragment_index[0]
    anchor_now = lax.dynamic_index_in_dim(anchor, frag_pick, 0, keepdims=False)
    moment_now = lax.dynamic_index_in_dim(momentum, frag_pick, 0, keepdims=False)
    replica_now = lax.dynamic_index_in_dim(replica_frag[0], frag_pick, 0, keepdims=False).astype(
        jnp.float32
    )
    replicas = lax.axis_size("rep")
    drift = anchor_now - replica_now

    def add_half(drift, bit):
        return drift + lax.ppermute(drift, "rep", [(r, r ^ bit) for r in range(replicas)])

    block = jax.ShapeDtypeStruct((rows, 2 * WIDE), jnp.bfloat16)
    *acts, inv, kept = pl.pallas_call(
        prepare_kernel,
        out_shape=(block,) * NY
        + (jax.ShapeDtypeStruct((rows, 1), jnp.float32), jax.ShapeDtypeStruct(shard.shape, shard.dtype)),
        compiler_params=params,
        cost_estimate=pl.CostEstimate(flops=2**21, bytes_accessed=4 * MIB, transcendentals=128),
        name="prepare",
    )(tokens, kv_cotangent, shard)

    far = send(shard, to_z(2, 4))
    act1 = send(acts[1], to_y(1))
    act3 = send(acts[3], to_y(3))
    far, drift = tie((far, drift))
    pair = jnp.concatenate([kept, far], axis=0)
    more = send(pair, to_z(4, 2))
    pair, drift = tie((pair, drift))
    drift = add_half(drift, 2)
    drift, acts[2] = tie((drift, acts[2]))
    act2 = send(acts[2], to_y(2))
    more, drift, act1 = tie((more, drift, act1))
    first = jnp.concatenate([pair, more], axis=0)
    second = send(first, to_z(1, 1))
    first_sib = send(first, to_core)
    drift = add_half(drift, 4)
    second, first_sib, act2, act3, drift = tie((second, first_sib, act2, act3, drift))
    acts = [acts[0], act1, act2, act3]
    second_sib = send(second, to_core)
    scratch = [pltpu.VMEM((HALF, WIDE), jnp.bfloat16), pltpu.VMEM((NY * rows, HALF + WIDE), jnp.bfloat16)]
    kv_first, own_first, *grads_first = pl.pallas_call(
        first_kernel,
        out_shape=(
            jax.ShapeDtypeStruct((NY * rows, WIDE), jnp.float32),
            jax.ShapeDtypeStruct((rows, HALF), jnp.float32),
        )
        + (jax.ShapeDtypeStruct((rows, HALF), jnp.bfloat16),) * (NY - 1),
        scratch_shapes=scratch,
        compiler_params=params,
        cost_estimate=pl.CostEstimate(flops=2**30, bytes_accessed=8 * MIB, transcendentals=0),
        name="first_half",
    )(first, first_sib, *acts)
    own, *backs = pl.pallas_call(
        second_kernel,
        out_shape=(jax.ShapeDtypeStruct((rows, 2 * WIDE), jnp.float32),) + (block,) * (NY - 1),
        scratch_shapes=scratch,
        compiler_params=params,
        cost_estimate=pl.CostEstimate(flops=2**30, bytes_accessed=8 * MIB, transcendentals=0),
        name="second_half",
    )(second, second_sib, kv_first, *acts, own_first, *grads_first)
    drift, *backs = tie((drift, *backs))
    gots = [send(backs[n - 1], to_y(-n)) for n in (2, 1, 3)]
    drift = add_half(drift, 1)
    outer_grad = drift / replicas
    momentum_new = outer_momentum * moment_now + outer_grad
    anchor_new = anchor_now - outer_rate * (outer_grad + outer_momentum * momentum_new)
    kv_part, inner = pl.pallas_call(
        begin_kernel,
        out_shape=(
            jax.ShapeDtypeStruct((rows, WIDE), jnp.float32),
            jax.ShapeDtypeStruct((rows, 1), jnp.float32),
        ),
        compiler_params=params,
        cost_estimate=pl.CostEstimate(flops=2**21, bytes_accessed=3 * MIB, transcendentals=0),
        name="begin",
    )(tokens, inv, own, gots[0])
    key_value, input_grad = pl.pallas_call(
        finish_kernel,
        out_shape=(
            jax.ShapeDtypeStruct((rows, WIDE), jnp.bfloat16),
            jax.ShapeDtypeStruct((rows, width), jnp.bfloat16),
        ),
        compiler_params=params,
        cost_estimate=pl.CostEstimate(flops=2**22, bytes_accessed=5 * MIB, transcendentals=0),
        name="finish",
    )(tokens, inv, kv_part, inner, own, *gots)
    return key_value, input_grad, anchor_new, momentum_new


def solution(mesh):
    return jax.shard_map(
        local,
        mesh=mesh,
        in_specs=(
            P(("rep", "fsdp"), None),
            P("rep", "fsdp", None),
            P(("rep", "fsdp"), None),
            P(),
            P(None, "fsdp"),
            P(None, "fsdp"),
            P("rep", None, "fsdp"),
        ),
        out_specs=(P(("rep", "fsdp"), None), P(("rep", "fsdp"), None), P("fsdp"), P("fsdp")),
        check_vma=False,
    )
```

```python
import jax
import jax.numpy as jnp
from jax import lax
from jax.experimental import pallas as pl
from jax.experimental.pallas import tpu as pltpu
from jax.sharding import PartitionSpec as P

norm_eps = 1e-05
outer_momentum = 0.9
outer_rate = 0.7

NY, NZ, NC = 4, 8, 2
EVEN = ((0, 2, 4, 6), (0, 4, 2, 6))
ODD = ((1, 3, 5, 7), (1, 5, 3, 7))
WIDE = 1024
HALF = WIDE // 2
MIB = 1 << 20


def device_pairs(move):
    pairs = []
    for y in range(NY):
        for z in range(NZ):
            for c in range(NC):
                to_y, to_z, to_c = move(y, z, c)
                pairs.append(((y * NZ + z) * NC + c, ((to_y % NY) * NZ + to_z) * NC + to_c))
    return pairs


def to_z(*bits):
    return device_pairs(lambda y, z, c: (y, z ^ bits[c], c))


def to_y(step):
    return device_pairs(lambda y, z, c: (y + step, z, c))


to_core = device_pairs(lambda y, z, c: (y, z, 1 - c))


def send(x, pairs):
    return lax.ppermute(x, "fsdp", pairs)


def place():
    me = lax.axis_index("fsdp")
    return me // (NZ * NC), lax.rem(me // NC, NZ), lax.rem(me, NC)


def slab(y, step):
    return pl.ds(pl.multiple_of(lax.rem(y + step, NY) * WIDE, WIDE), WIDE)


def prepare_kernel(tok_ref, cot_ref, shard_ref, *refs):
    outs, inv_ref, kept_ref = refs[:NY], refs[NY], refs[NY + 1]
    y, _, _ = place()
    kept_ref[...] = shard_ref[...]
    x = tok_ref[...].astype(jnp.float32)
    inv = lax.rsqrt(jnp.mean(x * x, axis=1, keepdims=True) + norm_eps)
    inv_ref[...] = inv
    for step, out_ref in enumerate(outs):
        out_ref[:, :WIDE] = (tok_ref[:, slab(y, step)].astype(jnp.float32) * inv).astype(jnp.bfloat16)
        out_ref[:, WIDE:] = cot_ref[...]


def half_of_features(mine_ref, sib_ref, order, acts, weight_ref, lhs_ref):
    _, z, c = place()
    rows = acts[0].shape[0]
    for sib, ref in enumerate((mine_ref, sib_ref)):
        core = lax.rem(c + sib, NC)
        for i in range(4):
            chip = jnp.bitwise_xor(z, jnp.where(core == 0, order[0][i], order[1][i]))
            at = pl.multiple_of(chip // 2 * 128 + core * 64, 64)
            weight_ref[pl.ds(at, 64)] = ref[64 * i : 64 * (i + 1)]
    odd = lax.rem(z + order[0][0], 2)
    for n, ref in enumerate(acts):
        lhs_ref[rows * n : rows * (n + 1), HALF:] = ref[:, WIDE:]
        for i in range(4):
            cols = pl.ds(pl.multiple_of((2 * i + odd) * 128, 128), 128)
            lhs_ref[rows * n : rows * (n + 1), 128 * i : 128 * (i + 1)] = ref[:, cols]


def first_kernel(mine_ref, sib_ref, *refs):
    acts, (kv_ref, own_ref, *outs), (weight_ref, lhs_ref) = refs[:NY], refs[NY:-2], refs[-2:]
    rows = acts[0].shape[0]
    half_of_features(mine_ref, sib_ref, EVEN, acts, weight_ref, lhs_ref)
    for i in range(HALF // 256):
        cols = slice(256 * i, 256 * (i + 1))
        part = lax.dot_general(
            lhs_ref[:, HALF:], weight_ref[cols], (((1,), (1,)), ((), ())), preferred_element_type=jnp.float32
        )
        own_ref[:, cols] = part[:rows]
        for n, out_ref in enumerate(outs, 1):
            out_ref[:, cols] = part[rows * n : rows * (n + 1)].astype(jnp.bfloat16)
    for i in range(WIDE // 256):
        cols = slice(256 * i, 256 * (i + 1))
        kv_ref[:, cols] = jnp.dot(lhs_ref[:, :HALF], weight_ref[:, cols], preferred_element_type=jnp.float32)


def second_kernel(mine_ref, sib_ref, kv_ref, *refs):
    acts, firsts, (own_ref, *outs), (weight_ref, lhs_ref) = (
        refs[:NY], refs[NY : 2 * NY], refs[2 * NY : -2], refs[-2:]
    )
    _, z, _ = place()
    rows = acts[0].shape[0]
    half_of_features(mine_ref, sib_ref, ODD, acts, weight_ref, lhs_ref)
    for i in range(WIDE // 256):
        cols = slice(256 * i, 256 * (i + 1))
        part = kv_ref[:, cols] + jnp.dot(
            lhs_ref[:, :HALF], weight_ref[:, cols], preferred_element_type=jnp.float32
        )
        own_ref[:, cols] = part[:rows]
        for n, out_ref in enumerate(outs, 1):
            out_ref[:, cols] = part[rows * n : rows * (n + 1)].astype(jnp.bfloat16)
    even, odd = lax.rem(z, 2), lax.rem(z + 1, 2)
    for i in range(HALF // 128):
        cols = pl.ds(pl.multiple_of(WIDE + (2 * i + even) * 128, 128), 128)
        for out_ref, first_ref in zip((own_ref, *outs), firsts):
            out_ref[:, cols] = first_ref[:, 128 * i : 128 * (i + 1)]
    for i in range(HALF // 256):
        part = lax.dot_general(
            lhs_ref[:, HALF:],
            weight_ref[256 * i : 256 * (i + 1)],
            (((1,), (1,)), ((), ())),
            preferred_element_type=jnp.float32,
        )
        for k in range(2):
            cols = pl.ds(pl.multiple_of(WIDE + (4 * i + 2 * k + odd) * 128, 128), 128)
            turn = part[:, 128 * k : 128 * (k + 1)]
            own_ref[:, cols] = turn[:rows]
            for n, out_ref in enumerate(outs, 1):
                out_ref[:, cols] = turn[rows * n : rows * (n + 1)].astype(jnp.bfloat16)


def begin_kernel(tok_ref, own_ref, across_ref, kv_ref, inner_ref):
    y, _, _ = place()
    kv_ref[...] = own_ref[:, :WIDE] + across_ref[:, :WIDE].astype(jnp.float32)
    inner = 0.0
    for step, ref in ((0, own_ref), (2, across_ref)):
        tok = tok_ref[:, slab(y, step)].astype(jnp.float32)
        inner += jnp.sum(ref[:, WIDE:].astype(jnp.float32) * tok, axis=1, keepdims=True)
    inner_ref[...] = inner


def finish_kernel(tok_ref, inv_ref, kv_part_ref, inner_ref, own_ref, *refs):
    gots, (kv_ref, grad_ref) = refs[: NY - 1], refs[NY - 1 :]
    y, _, _ = place()
    inv = inv_ref[...]
    kv = kv_part_ref[...]
    for ref in gots[1:]:
        kv += ref[:, :WIDE].astype(jnp.float32)
    kv_ref[...] = kv.astype(jnp.bfloat16)
    sources = list(zip((0, 2, 1, 3), (own_ref, *gots)))
    inner = inner_ref[...]
    for step, ref in sources[2:]:
        tok = tok_ref[:, slab(y, step)].astype(jnp.float32)
        inner += jnp.sum(ref[:, WIDE:].astype(jnp.float32) * tok, axis=1, keepdims=True)
    scale = inv * inv * (inv * inner / tok_ref.shape[1])
    for step, ref in sources:
        tok = tok_ref[:, slab(y, step)].astype(jnp.float32)
        grad = ref[:, WIDE:].astype(jnp.float32)
        grad_ref[:, slab(y, step)] = (inv * grad - tok * scale).astype(jnp.bfloat16)


def local(tokens, kv_weight, kv_cotangent, fragment_index, anchor, momentum, replica_frag):
    rows, width = tokens.shape
    shard = kv_weight[0]
    tie = lax.optimization_barrier
    params = pltpu.CompilerParams(vmem_limit_bytes=24 * MIB)

    frag_pick = fragment_index[0]
    anchor_now = lax.dynamic_index_in_dim(anchor, frag_pick, 0, keepdims=False)
    moment_now = lax.dynamic_index_in_dim(momentum, frag_pick, 0, keepdims=False)
    replica_now = lax.dynamic_index_in_dim(replica_frag[0], frag_pick, 0, keepdims=False).astype(
        jnp.float32
    )
    replicas = lax.axis_size("rep")
    drift = anchor_now - replica_now

    def add_half(drift, bit):
        return drift + lax.ppermute(drift, "rep", [(r, r ^ bit) for r in range(replicas)])

    block = jax.ShapeDtypeStruct((rows, 2 * WIDE), jnp.bfloat16)
    *acts, inv, kept = pl.pallas_call(
        prepare_kernel,
        out_shape=(block,) * NY
        + (jax.ShapeDtypeStruct((rows, 1), jnp.float32), jax.ShapeDtypeStruct(shard.shape, shard.dtype)),
        compiler_params=params,
        cost_estimate=pl.CostEstimate(flops=2**21, bytes_accessed=4 * MIB, transcendentals=128),
        name="prepare",
    )(tokens, kv_cotangent, shard)

    far = send(shard, to_z(2, 4))
    act1 = send(acts[1], to_y(1))
    act3 = send(acts[3], to_y(3))
    far, drift = tie((far, drift))
    pair = jnp.concatenate([kept, far], axis=0)
    more = send(pair, to_z(4, 2))
    pair, drift = tie((pair, drift))
    drift = add_half(drift, 2)
    drift, acts[2] = tie((drift, acts[2]))
    act2 = send(acts[2], to_y(2))
    more, drift, act1 = tie((more, drift, act1))
    first = jnp.concatenate([pair, more], axis=0)
    second = send(first, to_z(1, 1))
    first_sib = send(first, to_core)
    drift = add_half(drift, 4)
    second, first_sib, act2, act3, drift = tie((second, first_sib, act2, act3, drift))
    acts = [acts[0], act1, act2, act3]
    second_sib = send(second, to_core)
    scratch = [pltpu.VMEM((HALF, WIDE), jnp.bfloat16), pltpu.VMEM((NY * rows, HALF + WIDE), jnp.bfloat16)]
    kv_first, own_first, *grads_first = pl.pallas_call(
        first_kernel,
        out_shape=(
            jax.ShapeDtypeStruct((NY * rows, WIDE), jnp.float32),
            jax.ShapeDtypeStruct((rows, HALF), jnp.float32),
        )
        + (jax.ShapeDtypeStruct((rows, HALF), jnp.bfloat16),) * (NY - 1),
        scratch_shapes=scratch,
        compiler_params=params,
        cost_estimate=pl.CostEstimate(flops=2**30, bytes_accessed=8 * MIB, transcendentals=0),
        name="first_half",
    )(first, first_sib, *acts)
    own, *backs = pl.pallas_call(
        second_kernel,
        out_shape=(jax.ShapeDtypeStruct((rows, 2 * WIDE), jnp.float32),) + (block,) * (NY - 1),
        scratch_shapes=scratch,
        compiler_params=params,
        cost_estimate=pl.CostEstimate(flops=2**30, bytes_accessed=8 * MIB, transcendentals=0),
        name="second_half",
    )(second, second_sib, kv_first, *acts, own_first, *grads_first)
    drift, *backs = tie((drift, *backs))
    gots = [send(backs[n - 1], to_y(-n)) for n in (2, 1, 3)]
    drift = add_half(drift, 1)
    outer_grad = drift / replicas
    momentum_new = outer_momentum * moment_now + outer_grad
    anchor_new = anchor_now - outer_rate * (outer_grad + outer_momentum * momentum_new)
    kv_part, inner = pl.pallas_call(
        begin_kernel,
        out_shape=(
            jax.ShapeDtypeStruct((rows, WIDE), jnp.float32),
            jax.ShapeDtypeStruct((rows, 1), jnp.float32),
        ),
        compiler_params=params,
        cost_estimate=pl.CostEstimate(flops=2**21, bytes_accessed=3 * MIB, transcendentals=0),
        name="begin",
    )(tokens, own, gots[0])
    key_value, input_grad = pl.pallas_call(
        finish_kernel,
        out_shape=(
            jax.ShapeDtypeStruct((rows, WIDE), jnp.bfloat16),
            jax.ShapeDtypeStruct((rows, width), jnp.bfloat16),
        ),
        compiler_params=params,
        cost_estimate=pl.CostEstimate(flops=2**22, bytes_accessed=5 * MIB, transcendentals=0),
        name="finish",
    )(tokens, inv, kv_part, inner, own, *gots)
    return key_value, input_grad, anchor_new, momentum_new


def solution(mesh):
    return jax.shard_map(
        local,
        mesh=mesh,
        in_specs=(
            P(("rep", "fsdp"), None),
            P("rep", "fsdp", None),
            P(("rep", "fsdp"), None),
            P(),
            P(None, "fsdp"),
            P(None, "fsdp"),
            P("rep", None, "fsdp"),
        ),
        out_specs=(P(("rep", "fsdp"), None), P(("rep", "fsdp"), None), P("fsdp"), P("fsdp")),
        check_vma=False,
    )
```
